32 devices in a mesh: branch: 2 (over core), member: 4 (over z), expert: 4 (over y, x).
Axes of the slice: x: 2, y: 2, z: 4, core: 2. Of those that a mesh axis runs over, the one named last changes fastest.
Arguments:
- latents: bfloat16 [2, 16, 256, 4096], P('branch', ('member', 'expert')), may hold values from -6 to 6
- routes: int32 [2, 16, 256, 2], P('branch', ('member', 'expert')), may hold values from 0 to 3, all different within a row; in each aligned block of 256 rows (0 to 255, 256 to 511, ..., all dimensions but the last counted through in order) at most 160 rows name the same one
- keep_mask: int32 [2, 16, 256, 2], P('branch', ('member', 'expert')), may hold values 0 or 1
- router: bfloat16 [4096, 4], replicated, may hold values from -0.09375 to 0.09375
- expert_in: bfloat16 [4, 4096, 1280], P('expert', None, 'branch'), may hold values from -0.09375 to 0.09375
- expert_out: bfloat16 [4, 1280, 4096], P('expert', 'branch'), may hold values from -0.15625 to 0.15625
Outputs:
- guided: bfloat16 [16, 256, 4096], P(('member', 'expert'), None, 'branch')
The draws below stay inside these ranges and needn't reach their ends.
Inputs may be any that keep to these rules, and one draw needn't show every extreme that they name: The two experts of a token differ. Within each block of 256 tokens (the tokens of one device), no expert is named by more than 160 routes, a bound that some block reaches.
All inputs are finite; a program needn't handle non-finite values. No bound on the sum of `keep_mask` on one device may be relied on, other than what follows from the above.
Results may differ from the reference program's by a relative error of at most 0.0066.
Values may be sent and summed in bfloat16 or wider, within the bound.
A program may use at most 128 MiB of HBM per device.

```python
import math
import jax
import jax.numpy as jnp
import numpy as np
from jax import lax

D = 4096
FF = 1280
TOP = 2
SEQ = 256
MEM_DEV = 1
EXPERTS = 4
MEMBERS = 16
CAP = 160


def set_ends(result, key, low, top_value):
    shape = result.shape
    index_at = [jax.random.randint(jax.random.fold_in(key, axis), (), 0, shape[axis]) for axis in range(len(shape))]
    result = result.at[tuple(index_at)].set(low)
    longest = shape.index(max(shape))
    index_at[longest] = (index_at[longest] + 1) % shape[longest]
    return result.at[tuple(index_at)].set(top_value)


def shard_levels(key, extent, shards, low, top_value):
    def one(dim, shards_of):
        heights = jax.random.uniform(jax.random.fold_in(jax.random.fold_in(key, 6), dim), (shards_of,), jnp.float32, low / len(shards), top_value / len(shards))
        return jnp.repeat(jnp.exp(heights), extent[dim] // shards_of).reshape((-1,) + (1,) * (len(extent) - dim - 1))

    level = one(*shards[0])
    for cut in shards[1:]:
        level = level * one(*cut)
    return level


def deal_out(own_key, own, number, rows, count, top, most, slope):
    ranking = jax.random.permutation(own_key, count)
    packed, usual = portions_of(count, rows * top, most, slope, True), portions_of(count, rows * top, most, slope, False)
    places = jnp.arange(count)

    def named(tallies, offset_by):
        used = int((tallies > 0).sum())
        fixed = max(1, used // 4)
        passed = fixed + (places - fixed + offset_by * (used - fixed)) % max(1, count - fixed)
        return jnp.zeros((count,), jnp.int32).at[ranking[jnp.where(places < fixed, places, passed)]].set(jnp.asarray(tallies, jnp.int32))

    tallies = jnp.where(number % 4 == 0, named(packed, number // 4), named(usual, number - number // 4 - 1))
    mixed = jax.random.permutation(jax.random.fold_in(own, 3), count)
    source_of, sink = mixed[0:count // 2 * 2:2], mixed[1:count // 2 * 2:2]
    margin = jnp.minimum(tallies[source_of] - 1, most - tallies[sink]) // 2
    margin = jnp.where((source_of == ranking[0]) | (sink == ranking[0]) | (tallies[sink] == 0), 0, jnp.maximum(margin, 0))
    passed = jax.random.randint(jax.random.fold_in(own, 4), (count // 2,), 0, 1 << 20) % (margin + 1)
    tallies = tallies.at[source_of].add(-passed).at[sink].add(passed)
    members = jnp.searchsorted(jnp.cumsum(tallies), jnp.arange(rows * top), side="right").astype(jnp.int32)
    listing = members.reshape(top, rows).T
    listing = listing[jax.random.permutation(jax.random.fold_in(own, 1), rows)]
    offset_by = jax.random.randint(jax.random.fold_in(own, 2), (rows, 1), 0, top)
    return jnp.take_along_axis(listing, (jnp.arange(top)[None, :] + offset_by) % top, axis=1)


def portions_of(amount, total, reach, lean, full):
    portions = [(1 << 20) // math.isqrt(grade ** lean) + 1 for grade in range(1, amount + 1)]
    largest = reach if full else min(reach, max(-(-total // amount), total * portions[0] // sum(portions)))
    least = 1 if total - largest >= amount - 1 else 0
    counts, rest = [largest] + [least] * (amount - 1), total - largest - least * (amount - 1)
    while rest > 0:
        free = [i for i in range(1, amount) if counts[i] < largest] or [i for i in range(1, amount) if counts[i] < reach]
        whole, left = sum([portions[i] for i in free]), rest
        for i in free:
            addition = min(reach - counts[i], max(1, left * portions[i] // whole), rest)
            counts[i] = counts[i] + addition
            rest = rest - addition
    return np.array(counts)


def normal_values(rng, dims, width, reach, cuts=(), held_as=jnp.bfloat16):
    values = jax.random.normal(rng, dims, jnp.float32) * width
    if len(cuts) > 0:
        values = shard_levels(rng, dims, cuts, -0.22, 0.18) * values
    return jnp.clip(values, min=-reach, max=reach).astype(held_as)


def setup_inputs(seed: int = 0) -> dict:
    splits = jax.random.split(jax.random.key(seed), 7)
    latents = normal_values(splits[0], (2, MEMBERS, SEQ, D), 1.0, 6.0, ((0, 2), (1, 16)))
    routes_keys = jax.random.split(jax.random.fold_in(splits[1], 1), 2 * MEMBERS * SEQ // (MEM_DEV * SEQ))
    routes_turns = jax.random.permutation(jax.random.fold_in(splits[1], 3), 2 * MEMBERS * SEQ // (MEM_DEV * SEQ))
    routes = jax.vmap(lambda own, number: deal_out(jax.random.fold_in(splits[1], 2), own, number, MEM_DEV * SEQ, EXPERTS, TOP, CAP, 2))(routes_keys, routes_turns).reshape((2, MEMBERS, SEQ, TOP))
    keep_mask = set_ends((jax.random.randint(splits[2], (2, MEMBERS, SEQ, TOP), 0, 8) < 7).astype(jnp.int32), jax.random.fold_in(splits[2], 1), 0, 1)
    router = normal_values(splits[3], (D, EXPERTS), D ** -0.5, 0.09375)
    expert_in = normal_values(splits[4], (EXPERTS, D, FF), D ** -0.5, 0.09375, ((0, 4), (2, 2)))
    expert_out = normal_values(splits[5], (EXPERTS, FF, D), FF ** -0.5, 0.15625, ((0, 4), (1, 2)))
    return {"latents": latents, "routes": routes, "keep_mask": keep_mask, "router": router, "expert_in": expert_in, "expert_out": expert_out}


guidance_scale = 4.0


def reference(latents, routes, keep_mask, router, expert_in, expert_out):
    tok_count = MEM_DEV * SEQ
    blocks = 2 * MEMBERS // MEM_DEV
    tokens_all = latents.reshape(blocks, tok_count, D)
    routes_all = routes.reshape(blocks, tok_count * TOP)
    keep_all = keep_mask.reshape(blocks, tok_count * TOP)
    weight_in = expert_in.astype(jnp.float32)
    weight_out = expert_out.astype(jnp.float32)
    expert_ids = jnp.arange(EXPERTS, dtype=jnp.int32)

    def one_block(inputs):
        tokens, chosen, kept = inputs
        logits = jnp.dot(tokens, router, preferred_element_type=jnp.float32)
        picked = chosen.reshape(tok_count, TOP)[:, :, None] == expert_ids[None, None, :]
        score = jax.nn.sigmoid(jnp.sum(jnp.where(picked, logits[:, None, :], 0.0), axis=-1))
        gates = score / jnp.sum(score, axis=1, keepdims=True)
        onehot = ((chosen[:, None] == expert_ids[None, :]) & (kept[:, None] == 1)).astype(jnp.int32)
        before = jnp.cumsum(onehot, axis=0) - onehot
        slot = jnp.sum(before * onehot, axis=1).astype(jnp.int32)
        position = jnp.where(kept == 1, chosen * CAP + slot, EXPERTS * CAP).astype(jnp.int32)
        source = jnp.repeat(tokens, TOP, axis=0)
        buffer = jnp.zeros((EXPERTS * CAP, D), jnp.bfloat16).at[position].set(source, mode="drop")
        buffer = buffer.reshape(EXPERTS, CAP, D).astype(jnp.float32)
        hidden = jax.nn.gelu(jnp.einsum("ecd,edf->ecf", buffer, weight_in), approximate=True)
        hidden = lax.optimization_barrier(hidden.astype(jnp.bfloat16)).astype(jnp.float32)
        rows = jnp.einsum("ecf,efd->ecd", hidden, weight_out)
        rows = lax.optimization_barrier(rows.astype(jnp.bfloat16)).astype(jnp.float32)
        flat_rows = rows.reshape(EXPERTS * CAP, D)
        taken = flat_rows[jnp.minimum(position, EXPERTS * CAP - 1)]
        scale_rows = gates.reshape(tok_count * TOP) * kept.astype(jnp.float32)
        mixed = jnp.sum((taken * scale_rows[:, None]).reshape(tok_count, TOP, D), axis=1)
        return mixed.astype(jnp.bfloat16)

    moe = lax.map(one_block, (tokens_all, routes_all, keep_all)).reshape(2, MEMBERS, SEQ, D)
    cond = moe[0].astype(jnp.float32)
    uncond = moe[1].astype(jnp.float32)
    return (uncond + guidance_scale * (cond - uncond)).astype(jnp.bfloat16)
```

```python
import functools

import jax
import jax.numpy as jnp
from jax import lax
from jax.experimental import pallas as pl
from jax.experimental.pallas import tpu as pltpu
from jax.sharding import PartitionSpec as P

TOP = 2
guidance_scale = 4.0
MESH = pl.DeviceIdType.MESH
NO_SLOT = -4096.0
TILE = 256


def layer(
    experts,
    slots,
    tokens,
    routes,
    keep,
    router,
    w_in,
    w_out,
    guided,
    win,
    wout,
    meta,
    meta_in,
    meta_other,
    rows,
    rows_in,
    hid,
    mixed,
    own,
    part,
    part_in,
    weight_sem,
    meta_send,
    meta_recv,
    row_send,
    row_recv,
    hid_send,
    hid_recv,
    mo_send,
    mo_recv,
    part_send,
    part_recv,
):
    me = lax.axis_index("expert")
    branch = lax.axis_index("branch")
    other = 1 - branch
    count, width = tokens.shape
    half_units = w_in.shape[1]
    units = win.shape[1]
    half_width = guided.shape[1]
    slot_rows = rows.shape[1]

    barrier = pltpu.get_barrier_semaphore()
    for p in range(1, experts):
        pl.semaphore_signal(
            barrier, inc=1, device_id={"expert": me ^ p}, device_id_type=MESH
        )
    pl.semaphore_signal(barrier, inc=1, device_id={"branch": other}, device_id_type=MESH)
    pl.semaphore_wait(barrier, experts)

    unit_at = pl.multiple_of(branch * half_units, 128)
    mine_at = pl.multiple_of(branch * half_width, 128)
    theirs_at = pl.multiple_of(other * half_width, 128)
    in_here = pltpu.make_async_copy(
        w_in, win.at[:, pl.ds(unit_at, half_units)], weight_sem.at[0]
    )
    out_here = pltpu.make_async_copy(
        w_out.at[:, pl.ds(mine_at, half_width)],
        wout.at[pl.ds(unit_at, half_units), :],
        weight_sem.at[1],
    )
    in_there = pltpu.make_async_remote_copy(
        src_ref=w_in,
        dst_ref=win.at[:, pl.ds(unit_at, half_units)],
        send_sem=weight_sem.at[2],
        recv_sem=weight_sem.at[3],
        device_id={"branch": other},
        device_id_type=MESH,
    )
    out_there = pltpu.make_async_remote_copy(
        src_ref=w_out.at[:, pl.ds(theirs_at, half_width)],
        dst_ref=wout.at[pl.ds(unit_at, half_units), :],
        send_sem=weight_sem.at[4],
        recv_sem=weight_sem.at[5],
        device_id={"branch": other},
        device_id_type=MESH,
    )
    in_here.start()
    in_there.start()
    out_here.start()
    out_there.start()

    logits = lax.dot_general(
        router[...], tokens[...], (((1,), (1,)), ((), ())), preferred_element_type=jnp.float32
    )
    ids = lax.broadcasted_iota(jnp.int32, (experts, count), 0)
    scores, hits = [], []
    for k in range(TOP):
        hit = routes[k : k + 1, :] == ids
        picked = jnp.sum(jnp.where(hit, logits, 0.0), axis=0, keepdims=True)
        scores.append(1.0 / (1.0 + jnp.exp(-picked)))
        hits.append(jnp.logical_and(hit, keep[k : k + 1, :] == 1))
    total = scores[0] + scores[1]
    scale = jnp.where(branch == 0, guidance_scale, 1.0 - guidance_scale)
    gate = sum(jnp.where(hits[k], scale * (scores[k] / total), 0.0) for k in range(TOP))
    kept = jnp.logical_or(hits[0], hits[1])
    earlier = (
        lax.broadcasted_iota(jnp.int32, (count, count), 0)
        < lax.broadcasted_iota(jnp.int32, (count, count), 1)
    ).astype(jnp.float32)
    slot = jnp.dot(
        kept.astype(jnp.float32).astype(jnp.bfloat16),
        earlier.astype(jnp.bfloat16),
        preferred_element_type=jnp.float32,
    )
    slot = jnp.where(kept, slot, NO_SLOT)
    for e in range(experts):
        meta[e, 0:1, :] = slot[e : e + 1, :]
        meta[e, 1:2, :] = gate[e : e + 1, :]
        meta[e, 2:8, :] = jnp.zeros((6, count), jnp.float32)

    def row_copy(p):
        return pltpu.make_async_remote_copy(
            src_ref=rows.at[p],
            dst_ref=rows_in.at[p],
            send_sem=row_send.at[p],
            recv_sem=row_recv.at[p],
            device_id={"expert": me ^ p},
            device_id_type=MESH,
        )

    def meta_copy(p):
        return pltpu.make_async_remote_copy(
            src_ref=meta.at[me ^ p],
            dst_ref=meta_in.at[p],
            send_sem=meta_send.at[p],
            recv_sem=meta_recv.at[p],
            device_id={"expert": me ^ p},
            device_id_type=MESH,
        )

    def other_meta(p):
        return pltpu.make_async_remote_copy(
            src_ref=meta_in.at[p],
            dst_ref=meta_other.at[p],
            send_sem=mo_send.at[p],
            recv_sem=mo_recv.at[p],
            device_id={"branch": other},
            device_id_type=MESH,
        )

    def hid_copy(p):
        return pltpu.make_async_remote_copy(
            src_ref=hid.at[p, pl.ds(0, slot_rows)],
            dst_ref=hid.at[p, pl.ds(slot_rows, slot_rows)],
            send_sem=hid_send.at[p],
            recv_sem=hid_recv.at[p],
            device_id={"branch": other},
            device_id_type=MESH,
        )

    def part_copy(p):
        return pltpu.make_async_remote_copy(
            src_ref=part.at[lax.rem(p, slots)],
            dst_ref=part_in.at[p],
            send_sem=part_send.at[p],
            recv_sem=part_recv.at[p],
            device_id={"expert": me ^ p},
            device_id_type=MESH,
        )

    def fill(p, into, at):
        slot_of = meta[me ^ p, 0:1, :]
        place = (
            lax.broadcasted_iota(jnp.int32, (slot_rows, count), 0).astype(jnp.float32) == slot_of
        )
        place = place.astype(jnp.float32).astype(jnp.bfloat16)

        @pl.loop(0, width // (2 * TILE))
        def _(n):
            cols = pl.ds(pl.multiple_of(n * 2 * TILE, 2 * TILE), 2 * TILE)
            into[at, :, cols] = jnp.dot(
                place, tokens[:, cols], preferred_element_type=jnp.float32
            ).astype(jnp.bfloat16)

    @pl.loop(1, experts)
    def _(p):
        fill(p, rows, p)
        row_copy(p).start()
        meta_copy(p).start()

    fill(0, rows_in, 0)
    meta_in[0] = meta[me]
    in_here.wait()
    in_there.wait()
    out_here.wait()
    out_there.wait()

    def hidden(p):
        other_meta(p).start()

        @pl.loop(0, units // TILE)
        def _(n):
            cols = pl.ds(pl.multiple_of(n * TILE, TILE), TILE)
            pre = jnp.dot(rows_in[p], win[:, cols], preferred_element_type=jnp.float32)
            hid[p, 0:slot_rows, cols] = jax.nn.gelu(pre, approximate=True).astype(jnp.bfloat16)

        hid_copy(p).start()

    def mix(p):
        other_meta(p).wait()
        hid_copy(p).wait()
        here = jnp.transpose(meta_in[p])
        there = jnp.transpose(meta_other[p])
        lane = lax.broadcasted_iota(jnp.int32, (count, 2 * slot_rows), 1).astype(jnp.float32)
        weight = jnp.where(lane == here[:, 0:1], here[:, 1:2], 0.0) + jnp.where(
            lane == there[:, 0:1] + slot_rows, there[:, 1:2], 0.0
        )
        high = weight.astype(jnp.bfloat16)
        low = (weight - high.astype(jnp.float32)).astype(jnp.bfloat16)

        @pl.loop(0, units // TILE)
        def _(n):
            cols = pl.ds(pl.multiple_of(n * TILE, TILE), TILE)
            both = hid[p, :, cols]
            mixed[:, cols] = (
                jnp.dot(high, both, preferred_element_type=jnp.float32)
                + jnp.dot(low, both, preferred_element_type=jnp.float32)
            ).astype(jnp.bfloat16)

    hidden(0)
    mix(0)

    @pl.loop(0, half_width // TILE)
    def _(n):
        cols = pl.ds(pl.multiple_of(n * TILE, TILE), TILE)
        own[:, cols] = jnp.dot(mixed[...], wout[:, cols], preferred_element_type=jnp.float32)

    @pl.loop(1, experts)
    def _(p):
        meta_copy(p).wait()
        row_copy(p).wait()
        hidden(p)
        mix(p)
        if experts > slots:

            @pl.when(p > slots)
            def _():
                part_copy(p - slots).wait_send()

        @pl.loop(0, half_width // TILE)
        def _(n):
            cols = pl.ds(pl.multiple_of(n * TILE, TILE), TILE)
            part[lax.rem(p, slots), :, cols] = jnp.dot(
                mixed[...], wout[:, cols], preferred_element_type=jnp.float32
            ).astype(jnp.bfloat16)

        part_copy(p).start()

    @pl.loop(1, experts)
    def _(p):
        if experts > slots:

            @pl.when(p >= experts - slots)
            def _():
                part_copy(p).wait_send()
        else:
            part_copy(p).wait_send()
        part_copy(p).wait_recv()
        if experts > 4:
            own[...] += part_in[p].astype(jnp.float32)

    if experts > 4:
        guided[...] = own[...].astype(jnp.bfloat16)
    else:

        @pl.loop(0, half_width // TILE)
        def _(n):
            cols = pl.ds(pl.multiple_of(n * TILE, TILE), TILE)
            total = own[:, cols]
            for p in range(1, experts):
                total = total + part_in[p, :, cols].astype(jnp.float32)
            guided[:, cols] = total.astype(jnp.bfloat16)


def on_device(latents, routes, keep_mask, router, expert_in, expert_out):
    width = latents.shape[-1]
    tokens = latents.reshape(-1, width)
    count = tokens.shape[0]
    experts = lax.axis_size("expert")
    branches = lax.axis_size("branch")
    capacity = 5 * count * TOP // (4 * experts)
    slot_rows = -(-capacity // 16) * 16
    half_units = expert_in.shape[2]
    units = half_units * branches
    half_width = width // branches
    slots = min(experts, 4)
    routes = routes.reshape(count, TOP).T
    keep_mask = keep_mask.reshape(count, TOP).T
    bf16, f32 = jnp.bfloat16, jnp.float32
    vmem = pl.BlockSpec(memory_space=pltpu.VMEM)
    hbm = pl.BlockSpec(memory_space=pl.ANY)
    dma = pltpu.SemaphoreType.DMA
    guided = pl.pallas_call(
        functools.partial(layer, experts, slots),
        out_shape=jax.ShapeDtypeStruct((count, half_width), bf16),
        in_specs=[vmem, vmem, vmem, vmem, hbm, hbm],
        out_specs=vmem,
        scratch_shapes=[
            pltpu.VMEM((width, units), bf16),
            pltpu.VMEM((units, half_width), bf16),
            pltpu.VMEM((experts, 8, count), f32),
            pltpu.VMEM((experts, 8, count), f32),
            pltpu.VMEM((experts, 8, count), f32),
            pltpu.VMEM((experts, slot_rows, width), bf16),
            pltpu.VMEM((experts, slot_rows, width), bf16),
            pltpu.VMEM((experts, 2 * slot_rows, units), bf16),
            pltpu.VMEM((count, units), bf16),
            pltpu.VMEM((count, half_width), f32),
            pltpu.VMEM((slots, count, half_width), bf16),
            pltpu.VMEM((experts, count, half_width), bf16),
            dma((6,)),
        ]
        + [dma((experts,))] * 10,
        compiler_params=pltpu.CompilerParams(
            collective_id=0, has_side_effects=True, vmem_limit_bytes=63 * 2**20
        ),
        cost_estimate=pl.CostEstimate(
            flops=13_000_000_000, bytes_accessed=20_000_000, transcendentals=1_000_000
        ),
    )(tokens, routes, keep_mask, router.T, expert_in[0], expert_out[0])
    return guided.reshape(latents.shape[1], latents.shape[2], half_width)


def solution(mesh):
    placed = (
        P("branch", ("member", "expert"), None, None),
        P("branch", ("member", "expert"), None, None),
        P("branch", ("member", "expert"), None, None),
        P(),
        P("expert", None, "branch"),
        P("expert", "branch", None),
    )
    return jax.shard_map(
        on_device,
        mesh=mesh,
        in_specs=placed,
        out_specs=P(("member", "expert"), None, "branch"),
        check_vma=False,
    )
```

```python
import functools

import jax
import jax.numpy as jnp
from jax import lax
from jax.experimental import pallas as pl
from jax.experimental.pallas import tpu as pltpu
from jax.sharding import PartitionSpec as P

TOP = 2
guidance_scale = 4.0
MESH = pl.DeviceIdType.MESH
NO_SLOT = -4096.0
TILE = 256


def find_slots(experts, branch, tokens, routes, keep, router, meta):
    count = tokens.shape[0]
    logits = lax.dot_general(
        router[...], tokens[...], (((1,), (1,)), ((), ())), preferred_element_type=jnp.float32
    )
    ids = lax.broadcasted_iota(jnp.int32, (experts, count), 0)
    scores, hits = [], []
    for k in range(TOP):
        hit = routes[k : k + 1, :] == ids
        picked = jnp.sum(jnp.where(hit, logits, 0.0), axis=0, keepdims=True)
        scores.append(1.0 / (1.0 + jnp.exp(-picked)))
        hits.append(jnp.logical_and(hit, keep[k : k + 1, :] == 1))
    total = scores[0] + scores[1]
    scale = jnp.where(branch == 0, guidance_scale, 1.0 - guidance_scale)
    gate = sum(jnp.where(hits[k], scale * (scores[k] / total), 0.0) for k in range(TOP))
    kept = jnp.logical_or(hits[0], hits[1])
    earlier = (
        lax.broadcasted_iota(jnp.int32, (count, count), 0)
        < lax.broadcasted_iota(jnp.int32, (count, count), 1)
    ).astype(jnp.float32)
    slot = jnp.dot(
        kept.astype(jnp.float32).astype(jnp.bfloat16),
        earlier.astype(jnp.bfloat16),
        preferred_element_type=jnp.float32,
    )
    slot = jnp.where(kept, slot, NO_SLOT)
    for e in range(experts):
        meta[e, 0:1, :] = slot[e : e + 1, :]
        meta[e, 1:2, :] = gate[e : e + 1, :]
        meta[e, 2:8, :] = jnp.zeros((6, count), jnp.float32)


def layer(
    experts,
    slots,
    tokens,
    routes,
    keep,
    router,
    w_in,
    w_out,
    guided,
    win,
    wout,
    meta,
    meta_in,
    meta_other,
    rows,
    rows_in,
    hid,
    mixed,
    own,
    part,
    part_in,
    weight_sem,
    meta_send,
    meta_recv,
    row_send,
    row_recv,
    hid_send,
    hid_recv,
    mo_send,
    mo_recv,
    part_send,
    part_recv,
):
    me = lax.axis_index("expert")
    branch = lax.axis_index("branch")
    other = 1 - branch
    count, width = tokens.shape
    half_units = w_in.shape[1]
    units = win.shape[1]
    half_width = guided.shape[1]
    slot_rows = rows.shape[1]

    barrier = pltpu.get_barrier_semaphore()
    for p in range(1, experts):
        pl.semaphore_signal(
            barrier, inc=1, device_id={"expert": me ^ p}, device_id_type=MESH
        )
    pl.semaphore_signal(barrier, inc=1, device_id={"branch": other}, device_id_type=MESH)
    pl.semaphore_wait(barrier, experts)

    unit_at = pl.multiple_of(branch * half_units, 128)
    mine_at = pl.multiple_of(branch * half_width, 128)
    theirs_at = pl.multiple_of(other * half_width, 128)
    in_here = pltpu.make_async_copy(
        w_in, win.at[:, pl.ds(unit_at, half_units)], weight_sem.at[0]
    )
    out_here = pltpu.make_async_copy(
        w_out.at[:, pl.ds(mine_at, half_width)],
        wout.at[pl.ds(unit_at, half_units), :],
        weight_sem.at[1],
    )
    in_there = pltpu.make_async_remote_copy(
        src_ref=w_in,
        dst_ref=win.at[:, pl.ds(unit_at, half_units)],
        send_sem=weight_sem.at[2],
        recv_sem=weight_sem.at[3],
        device_id={"branch": other},
        device_id_type=MESH,
    )
    out_there = pltpu.make_async_remote_copy(
        src_ref=w_out.at[:, pl.ds(theirs_at, half_width)],
        dst_ref=wout.at[pl.ds(unit_at, half_units), :],
        send_sem=weight_sem.at[4],
        recv_sem=weight_sem.at[5],
        device_id={"branch": other},
        device_id_type=MESH,
    )
    in_here.start()
    in_there.start()
    out_here.start()
    out_there.start()

    find_slots(experts, branch, tokens, routes, keep, router, meta)

    def row_copy(p):
        return pltpu.make_async_remote_copy(
            src_ref=rows.at[p],
            dst_ref=rows_in.at[p],
            send_sem=row_send.at[p],
            recv_sem=row_recv.at[p],
            device_id={"expert": me ^ p},
            device_id_type=MESH,
        )

    def meta_copy(p):
        return pltpu.make_async_remote_copy(
            src_ref=meta.at[me ^ p],
            dst_ref=meta_in.at[p],
            send_sem=meta_send.at[p],
            recv_sem=meta_recv.at[p],
            device_id={"expert": me ^ p},
            device_id_type=MESH,
        )

    def other_meta(p):
        return pltpu.make_async_remote_copy(
            src_ref=meta_in.at[p],
            dst_ref=meta_other.at[p],
            send_sem=mo_send.at[p],
            recv_sem=mo_recv.at[p],
            device_id={"branch": other},
            device_id_type=MESH,
        )

    def hid_copy(p):
        return pltpu.make_async_remote_copy(
            src_ref=hid.at[p, pl.ds(0, slot_rows)],
            dst_ref=hid.at[p, pl.ds(slot_rows, slot_rows)],
            send_sem=hid_send.at[p],
            recv_sem=hid_recv.at[p],
            device_id={"branch": other},
            device_id_type=MESH,
        )

    def part_copy(p):
        return pltpu.make_async_remote_copy(
            src_ref=part.at[lax.rem(p, slots)],
            dst_ref=part_in.at[p],
            send_sem=part_send.at[p],
            recv_sem=part_recv.at[p],
            device_id={"expert": me ^ p},
            device_id_type=MESH,
        )

    def fill(p, into, at):
        slot_of = meta[me ^ p, 0:1, :]
        place = (
            lax.broadcasted_iota(jnp.int32, (slot_rows, count), 0).astype(jnp.float32) == slot_of
        )
        place = place.astype(jnp.float32).astype(jnp.bfloat16)

        @pl.loop(0, width // (2 * TILE))
        def _(n):
            cols = pl.ds(pl.multiple_of(n * 2 * TILE, 2 * TILE), 2 * TILE)
            into[at, :, cols] = jnp.dot(
                place, tokens[:, cols], preferred_element_type=jnp.float32
            ).astype(jnp.bfloat16)

    @pl.loop(1, experts)
    def _(p):
        fill(p, rows, p)
        row_copy(p).start()
        meta_copy(p).start()

    fill(0, rows_in, 0)
    meta_in[0] = meta[me]
    in_here.wait()
    in_there.wait()
    out_here.wait()
    out_there.wait()

    def hidden(p):
        other_meta(p).start()

        @pl.loop(0, units // TILE)
        def _(n):
            cols = pl.ds(pl.multiple_of(n * TILE, TILE), TILE)
            pre = jnp.dot(rows_in[p], win[:, cols], preferred_element_type=jnp.float32)
            hid[p, 0:slot_rows, cols] = jax.nn.gelu(pre, approximate=True).astype(jnp.bfloat16)

        hid_copy(p).start()

    def mix(p):
        other_meta(p).wait()
        hid_copy(p).wait()
        here = jnp.transpose(meta_in[p])
        there = jnp.transpose(meta_other[p])
        lane = lax.broadcasted_iota(jnp.int32, (count, 2 * slot_rows), 1).astype(jnp.float32)
        weight = jnp.where(lane == here[:, 0:1], here[:, 1:2], 0.0) + jnp.where(
            lane == there[:, 0:1] + slot_rows, there[:, 1:2], 0.0
        )
        high = weight.astype(jnp.bfloat16)
        low = (weight - high.astype(jnp.float32)).astype(jnp.bfloat16)

        @pl.loop(0, units // TILE)
        def _(n):
            cols = pl.ds(pl.multiple_of(n * TILE, TILE), TILE)
            both = hid[p, :, cols]
            mixed[:, cols] = (
                jnp.dot(high, both, preferred_element_type=jnp.float32)
                + jnp.dot(low, both, preferred_element_type=jnp.float32)
            ).astype(jnp.bfloat16)

    hidden(0)
    mix(0)

    @pl.loop(0, half_width // TILE)
    def _(n):
        cols = pl.ds(pl.multiple_of(n * TILE, TILE), TILE)
        own[:, cols] = jnp.dot(mixed[...], wout[:, cols], preferred_element_type=jnp.float32)

    @pl.loop(1, experts)
    def _(p):
        meta_copy(p).wait()
        row_copy(p).wait()
        hidden(p)
        mix(p)
        if experts > slots:

            @pl.when(p > slots)
            def _():
                part_copy(p - slots).wait_send()

        @pl.loop(0, half_width // TILE)
        def _(n):
            cols = pl.ds(pl.multiple_of(n * TILE, TILE), TILE)
            part[lax.rem(p, slots), :, cols] = jnp.dot(
                mixed[...], wout[:, cols], preferred_element_type=jnp.float32
            ).astype(jnp.bfloat16)

        part_copy(p).start()

    @pl.loop(1, experts)
    def _(p):
        if experts > slots:

            @pl.when(p >= experts - slots)
            def _():
                part_copy(p).wait_send()
        else:
            part_copy(p).wait_send()
        part_copy(p).wait_recv()
        if experts > 4:
            own[...] += part_in[p].astype(jnp.float32)

    if experts > 4:
        guided[...] = own[...].astype(jnp.bfloat16)
    else:

        @pl.loop(0, half_width // TILE)
        def _(n):
            cols = pl.ds(pl.multiple_of(n * TILE, TILE), TILE)
            total = own[:, cols]
            for p in range(1, experts):
                total = total + part_in[p, :, cols].astype(jnp.float32)
            guided[:, cols] = total.astype(jnp.bfloat16)


def layer_2x2(
    tokens,
    routes,
    keep,
    router,
    w_in,
    w_out,
    guided,
    win,
    wout,
    meta,
    meta_in,
    meta_other,
    rows,
    rows_in,
    half_in,
    hid,
    mixed,
    own,
    late,
    part,
    part_in,
    weight_sem,
    half_send,
    half_recv,
    meta_send,
    meta_recv,
    row_send,
    row_recv,
    hid_send,
    hid_recv,
    mo_send,
    mo_recv,
    part_send,
    part_recv,
):
    experts = 4
    me = lax.axis_index("expert")
    branch = lax.axis_index("branch")
    other = 1 - branch
    count, width = tokens.shape
    half_units = w_in.shape[1]
    units = win.shape[1]
    half_width = guided.shape[1]
    slot_rows = rows.shape[1]
    half = width // 2
    quarter = half_width // 2

    barrier = pltpu.get_barrier_semaphore()
    for p in range(1, experts):
        pl.semaphore_signal(
            barrier, inc=1, device_id={"expert": me ^ p}, device_id_type=MESH
        )
    pl.semaphore_signal(barrier, inc=1, device_id={"branch": other}, device_id_type=MESH)
    pl.semaphore_wait(barrier, experts)

    def to_expert(p, source, target, send, recv):
        return pltpu.make_async_remote_copy(
            src_ref=source,
            dst_ref=target,
            send_sem=send,
            recv_sem=recv,
            device_id={"expert": me ^ p},
            device_id_type=MESH,
        )

    def to_core(source, target, send, recv):
        return pltpu.make_async_remote_copy(
            src_ref=source,
            dst_ref=target,
            send_sem=send,
            recv_sem=recv,
            device_id={"branch": other},
            device_id_type=MESH,
        )

    def raw(p):
        return to_expert(
            p,
            tokens.at[:, pl.ds((p - 1) * half, half)],
            half_in.at[p - 1],
            half_send.at[p - 1],
            half_recv.at[p - 1],
        )

    raw(1).start()
    raw(2).start()

    unit_at = pl.multiple_of(branch * half_units, 128)
    mine_at = pl.multiple_of(branch * half_width, 128)
    theirs_at = pl.multiple_of(other * half_width, 128)
    weights = [
        pltpu.make_async_copy(w_in, win.at[:, pl.ds(unit_at, half_units)], weight_sem.at[0]),
        to_core(w_in, win.at[:, pl.ds(unit_at, half_units)], weight_sem.at[2], weight_sem.at[3]),
        pltpu.make_async_copy(
            w_out.at[:, pl.ds(mine_at, half_width)],
            wout.at[pl.ds(unit_at, half_units), :],
            weight_sem.at[1],
        ),
        to_core(
            w_out.at[:, pl.ds(theirs_at, half_width)],
            wout.at[pl.ds(unit_at, half_units), :],
            weight_sem.at[4],
            weight_sem.at[5],
        ),
    ]
    for copy in weights:
        copy.start()

    find_slots(experts, branch, tokens, routes, keep, router, meta)

    def meta_copy(p):
        return to_expert(p, meta, meta_in.at[p], meta_send.at[p], meta_recv.at[p])

    for p in range(1, experts):
        meta_copy(p).start()

    def fill(slot_of, source, source_at, into, at, into_at):
        place = (
            lax.broadcasted_iota(jnp.int32, (slot_rows, count), 0).astype(jnp.float32) == slot_of
        )
        place = place.astype(jnp.float32).astype(jnp.bfloat16)

        @pl.loop(0, half // (2 * TILE))
        def _(n):
            off = n * 2 * TILE
            cols = pl.ds(pl.multiple_of(source_at + off, 2 * TILE), 2 * TILE)
            out = pl.ds(pl.multiple_of(into_at + off, 2 * TILE), 2 * TILE)
            into[at, :, out] = jnp.dot(
                place, source[:, cols], preferred_element_type=jnp.float32
            ).astype(jnp.bfloat16)

    def direct(p):
        cols = pl.ds((2 - p) * half, half)
        return to_expert(
            p, rows.at[p, :, cols], rows_in.at[p, :, cols], row_send.at[p], row_recv.at[p]
        )

    def forward(p):
        cols = pl.ds((2 - p) * half, half)
        return to_expert(
            p, rows.at[3, :, cols], rows_in.at[3, :, cols], row_send.at[p + 2], row_recv.at[p + 2]
        )

    for p in (1, 2):
        fill(meta[me ^ p, 0:1, :], tokens, (2 - p) * half, rows, p, (2 - p) * half)
    for p in (1, 2):
        raw(p).wait_send()
        direct(p).start()
    for h in range(2):
        fill(meta[me, 0:1, :], tokens, h * half, rows_in, 0, h * half)
    for p in range(1, experts):
        meta_copy(p).wait()
    for p in (1, 2):
        raw(p).wait_recv()
        q = 3 - p
        fill(meta_in[p, me ^ q, 0:1, :], half_in.at[p - 1], 0, rows, 3, (p - 1) * half)
        fill(meta_in[p, me, 0:1, :], half_in.at[p - 1], 0, rows_in, p, (p - 1) * half)
    meta_in[0] = meta[...]

    def other_meta(p):
        return to_core(meta_in.at[p, me], meta_other.at[p], mo_send.at[p], mo_recv.at[p])

    def hid_copy(p):
        return to_core(
            hid.at[p, pl.ds(0, slot_rows)],
            hid.at[p, pl.ds(slot_rows, slot_rows)],
            hid_send.at[p],
            hid_recv.at[p],
        )

    for p in range(experts):
        other_meta(p).start()

    def hidden(p):
        @pl.loop(0, units // TILE)
        def _(n):
            cols = pl.ds(pl.multiple_of(n * TILE, TILE), TILE)
            pre = jnp.dot(rows_in[p], win[:, cols], preferred_element_type=jnp.float32)
            hid[p, 0:slot_rows, cols] = jax.nn.gelu(pre, approximate=True).astype(jnp.bfloat16)

        hid_copy(p).start()

    def mix(p, into):
        other_meta(p).wait()
        here = jnp.transpose(meta_in[p, me])
        there = jnp.transpose(meta_other[p])
        lane = lax.broadcasted_iota(jnp.int32, (count, 2 * slot_rows), 1).astype(jnp.float32)
        weight = jnp.where(lane == here[:, 0:1], here[:, 1:2], 0.0) + jnp.where(
            lane == there[:, 0:1] + slot_rows, there[:, 1:2], 0.0
        )
        high = weight.astype(jnp.bfloat16)
        low = (weight - high.astype(jnp.float32)).astype(jnp.bfloat16)
        hid_copy(p).wait()

        @pl.loop(0, units // TILE)
        def _(n):
            cols = pl.ds(pl.multiple_of(n * TILE, TILE), TILE)
            both = hid[p, :, cols]
            mixed[into, :, cols] = (
                jnp.dot(high, both, preferred_element_type=jnp.float32)
                + jnp.dot(low, both, preferred_element_type=jnp.float32)
            ).astype(jnp.bfloat16)

    def output(of, side, store):
        @pl.loop(0, quarter // TILE)
        def _(n):
            at = pl.multiple_of(n * TILE, TILE)
            cols = pl.ds(pl.multiple_of(side * quarter + at, TILE), TILE)
            store(
                cols,
                pl.ds(at, TILE),
                jnp.dot(mixed[of], wout[:, cols], preferred_element_type=jnp.float32),
            )

    def keep_own(cols, _, value):
        own[:, cols] = value

    def to_part(p):
        def store(cols, _, value):
            part[p, :, cols] = value.astype(jnp.bfloat16)

        return store

    def to_late(index):
        def store(_, cols, value):
            late[index, :, cols] = value

        return store

    def part_copy(p, side):
        index = {(1, 0): 0, (1, 1): 1, (2, 0): 2, (2, 1): 3, (3, 0): 4, (3, 1): 5}[p, side]
        cols = pl.ds(side * quarter, quarter)
        return to_expert(
            side + 1 if p == 3 else p,
            part.at[p, :, cols],
            part_in.at[p, :, cols],
            part_send.at[index],
            part_recv.at[index],
        )

    for copy in weights:
        copy.wait()
    hidden(0)
    mix(0, 0)
    for side in range(2):
        output(0, side, keep_own)
    forward(1).start()
    forward(2).start()
    for p in (1, 2):
        direct(p).wait()
        hidden(p)
    for p in (1, 2):
        mix(p, p)
        output(p, p - 1, to_part(p))
        part_copy(p, p - 1).start()
    for p in (1, 2):
        output(p, 2 - p, to_late(p - 1))
    for p in (1, 2):
        forward(p).wait()
    hidden(3)
    mix(3, 0)
    for side in range(2):
        output(0, side, to_part(3))
        part_copy(3, side).start()
    for side in range(2):
        p = 2 - side
        part_copy(3, side).wait()

        @pl.loop(0, quarter // TILE)
        def _(n):
            at = pl.multiple_of(n * TILE, TILE)
            cols = pl.ds(pl.multiple_of(side * quarter + at, TILE), TILE)
            part[p, :, cols] = (
                late[p - 1, :, pl.ds(at, TILE)] + part_in[3, :, cols].astype(jnp.float32)
            ).astype(jnp.bfloat16)

        part_copy(p, side).start()
    for p in (1, 2):
        part_copy(p, p - 1).wait()
    for side in range(2):
        part_copy(2 - side, side).wait()

        @pl.loop(0, quarter // TILE)
        def _(n):
            cols = pl.ds(pl.multiple_of(side * quarter + n * TILE, TILE), TILE)
            total = own[:, cols]
            for p in (1, 2):
                total = total + part_in[p, :, cols].astype(jnp.float32)
            guided[:, cols] = total.astype(jnp.bfloat16)


def on_device(latents, routes, keep_mask, router, expert_in, expert_out):
    width = latents.shape[-1]
    tokens = latents.reshape(-1, width)
    count = tokens.shape[0]
    experts = lax.axis_size("expert")
    branches = lax.axis_size("branch")
    capacity = 5 * count * TOP // (4 * experts)
    slot_rows = -(-capacity // 16) * 16
    half_units = expert_in.shape[2]
    units = half_units * branches
    half_width = width // branches
    slots = min(experts, 4)
    routes = routes.reshape(count, TOP).T
    keep_mask = keep_mask.reshape(count, TOP).T
    bf16, f32 = jnp.bfloat16, jnp.float32
    vmem = pl.BlockSpec(memory_space=pltpu.VMEM)
    hbm = pl.BlockSpec(memory_space=pl.ANY)
    dma = pltpu.SemaphoreType.DMA
    if experts == 4:
        kernel = layer_2x2
        shapes = [
            ((width, units), bf16),
            ((units, half_width), bf16),
            ((experts, 8, count), f32),
            ((experts, experts, 8, count), f32),
            ((experts, 8, count), f32),
            ((experts, slot_rows, width), bf16),
            ((experts, slot_rows, width), bf16),
            ((2, count, width // 2), bf16),
            ((experts, 2 * slot_rows, units), bf16),
            ((3, count, units), bf16),
            ((count, half_width), f32),
            ((2, count, half_width // 2), f32),
            ((experts, count, half_width), bf16),
            ((experts, count, half_width), bf16),
        ]
        semaphores = [6, 2, 2, 4, 4, 5, 5, 4, 4, 4, 4, 6, 6]
    else:
        kernel = functools.partial(layer, experts, slots)
        shapes = [
            ((width, units), bf16),
            ((units, half_width), bf16),
            ((experts, 8, count), f32),
            ((experts, 8, count), f32),
            ((experts, 8, count), f32),
            ((experts, slot_rows, width), bf16),
            ((experts, slot_rows, width), bf16),
            ((experts, 2 * slot_rows, units), bf16),
            ((count, units), bf16),
            ((count, half_width), f32),
            ((slots, count, half_width), bf16),
            ((experts, count, half_width), bf16),
        ]
        semaphores = [6] + [experts] * 10
    guided = pl.pallas_call(
        kernel,
        out_shape=jax.ShapeDtypeStruct((count, half_width), bf16),
        in_specs=[vmem, vmem, vmem, vmem, hbm, hbm],
        out_specs=vmem,
        scratch_shapes=[pltpu.VMEM(*s) for s in shapes] + [dma((s,)) for s in semaphores],
        compiler_params=pltpu.CompilerParams(
            collective_id=0, has_side_effects=True, vmem_limit_bytes=63 * 2**20
        ),
        cost_estimate=pl.CostEstimate(
            flops=13_000_000_000, bytes_accessed=20_000_000, transcendentals=1_000_000
        ),
    )(tokens, routes, keep_mask, router.T, expert_in[0], expert_out[0])
    return guided.reshape(latents.shape[1], latents.shape[2], half_width)


def solution(mesh):
    placed = (
        P("branch", ("member", "expert"), None, None),
        P("branch", ("member", "expert"), None, None),
        P("branch", ("member", "expert"), None, None),
        P(),
        P("expert", None, "branch"),
        P("expert", "branch", None),
    )
    return jax.shard_map(
        on_device,
        mesh=mesh,
        in_specs=placed,
        out_specs=P(("member", "expert"), None, "branch"),
        check_vma=False,
    )
```

```python
import functools

import jax
import jax.numpy as jnp
from jax import lax
from jax.experimental import pallas as pl
from jax.experimental.pallas import tpu as pltpu
from jax.sharding import PartitionSpec as P

TOP = 2
guidance_scale = 4.0
MESH = pl.DeviceIdType.MESH
NO_SLOT = -4096.0
TILE = 256
PIECES = 2


def find_slots(experts, branch, tokens, routes, keep, router, meta):
    count = tokens.shape[0]
    logits = lax.dot_general(
        router[...], tokens[...], (((1,), (1,)), ((), ())), preferred_element_type=jnp.float32
    )
    ids = lax.broadcasted_iota(jnp.int32, (experts, count), 0)
    scores, hits = [], []
    for k in range(TOP):
        hit = routes[k : k + 1, :] == ids
        picked = jnp.sum(jnp.where(hit, logits, 0.0), axis=0, keepdims=True)
        scores.append(1.0 / (1.0 + jnp.exp(-picked)))
        hits.append(jnp.logical_and(hit, keep[k : k + 1, :] == 1))
    total = scores[0] + scores[1]
    scale = jnp.where(branch == 0, guidance_scale, 1.0 - guidance_scale)
    gate = sum(jnp.where(hits[k], scale * (scores[k] / total), 0.0) for k in range(TOP))
    kept = jnp.logical_or(hits[0], hits[1])
    earlier = (
        lax.broadcasted_iota(jnp.int32, (count, count), 0)
        < lax.broadcasted_iota(jnp.int32, (count, count), 1)
    ).astype(jnp.float32)
    slot = jnp.dot(
        kept.astype(jnp.float32).astype(jnp.bfloat16),
        earlier.astype(jnp.bfloat16),
        preferred_element_type=jnp.float32,
    )
    slot = jnp.where(kept, slot, NO_SLOT)
    for e in range(experts):
        meta[e, 0:1, :] = slot[e : e + 1, :]
        meta[e, 1:2, :] = gate[e : e + 1, :]
        meta[e, 2:8, :] = jnp.zeros((6, count), jnp.float32)


def layer(
    experts,
    slots,
    tokens,
    routes,
    keep,
    router,
    w_in,
    w_out,
    guided,
    win,
    wout,
    meta,
    meta_in,
    meta_other,
    rows,
    rows_in,
    hid,
    mixed,
    own,
    part,
    part_in,
    weight_sem,
    meta_send,
    meta_recv,
    row_send,
    row_recv,
    hid_send,
    hid_recv,
    mo_send,
    mo_recv,
    part_send,
    part_recv,
):
    me = lax.axis_index("expert")
    branch = lax.axis_index("branch")
    other = 1 - branch
    count, width = tokens.shape
    half_units = w_in.shape[1]
    units = win.shape[1]
    half_width = guided.shape[1]
    slot_rows = rows.shape[1]

    barrier = pltpu.get_barrier_semaphore()
    for p in range(1, experts):
        pl.semaphore_signal(
            barrier, inc=1, device_id={"expert": me ^ p}, device_id_type=MESH
        )
    pl.semaphore_signal(barrier, inc=1, device_id={"branch": other}, device_id_type=MESH)
    pl.semaphore_wait(barrier, experts)

    unit_at = pl.multiple_of(branch * half_units, 128)
    mine_at = pl.multiple_of(branch * half_width, 128)
    theirs_at = pl.multiple_of(other * half_width, 128)
    in_here = pltpu.make_async_copy(
        w_in, win.at[:, pl.ds(unit_at, half_units)], weight_sem.at[0]
    )
    out_here = pltpu.make_async_copy(
        w_out.at[:, pl.ds(mine_at, half_width)],
        wout.at[pl.ds(unit_at, half_units), :],
        weight_sem.at[1],
    )
    in_there = pltpu.make_async_remote_copy(
        src_ref=w_in,
        dst_ref=win.at[:, pl.ds(unit_at, half_units)],
        send_sem=weight_sem.at[2],
        recv_sem=weight_sem.at[3],
        device_id={"branch": other},
        device_id_type=MESH,
    )
    out_there = pltpu.make_async_remote_copy(
        src_ref=w_out.at[:, pl.ds(theirs_at, half_width)],
        dst_ref=wout.at[pl.ds(unit_at, half_units), :],
        send_sem=weight_sem.at[4],
        recv_sem=weight_sem.at[5],
        device_id={"branch": other},
        device_id_type=MESH,
    )
    in_here.start()
    in_there.start()
    out_here.start()
    out_there.start()

    find_slots(experts, branch, tokens, routes, keep, router, meta)

    def row_copy(p):
        return pltpu.make_async_remote_copy(
            src_ref=rows.at[p],
            dst_ref=rows_in.at[p],
            send_sem=row_send.at[p],
            recv_sem=row_recv.at[p],
            device_id={"expert": me ^ p},
            device_id_type=MESH,
        )

    def meta_copy(p):
        return pltpu.make_async_remote_copy(
            src_ref=meta.at[me ^ p],
            dst_ref=meta_in.at[p],
            send_sem=meta_send.at[p],
            recv_sem=meta_recv.at[p],
            device_id={"expert": me ^ p},
            device_id_type=MESH,
        )

    def other_meta(p):
        return pltpu.make_async_remote_copy(
            src_ref=meta_in.at[p],
            dst_ref=meta_other.at[p],
            send_sem=mo_send.at[p],
            recv_sem=mo_recv.at[p],
            device_id={"branch": other},
            device_id_type=MESH,
        )

    def hid_copy(p):
        return pltpu.make_async_remote_copy(
            src_ref=hid.at[p, pl.ds(0, slot_rows)],
            dst_ref=hid.at[p, pl.ds(slot_rows, slot_rows)],
            send_sem=hid_send.at[p],
            recv_sem=hid_recv.at[p],
            device_id={"branch": other},
            device_id_type=MESH,
        )

    def part_copy(p):
        return pltpu.make_async_remote_copy(
            src_ref=part.at[lax.rem(p, slots)],
            dst_ref=part_in.at[p],
            send_sem=part_send.at[p],
            recv_sem=part_recv.at[p],
            device_id={"expert": me ^ p},
            device_id_type=MESH,
        )

    def fill(p, into, at):
        slot_of = meta[me ^ p, 0:1, :]
        place = (
            lax.broadcasted_iota(jnp.int32, (slot_rows, count), 0).astype(jnp.float32) == slot_of
        )
        place = place.astype(jnp.float32).astype(jnp.bfloat16)

        @pl.loop(0, width // (2 * TILE))
        def _(n):
            cols = pl.ds(pl.multiple_of(n * 2 * TILE, 2 * TILE), 2 * TILE)
            into[at, :, cols] = jnp.dot(
                place, tokens[:, cols], preferred_element_type=jnp.float32
            ).astype(jnp.bfloat16)

    @pl.loop(1, experts)
    def _(p):
        fill(p, rows, p)
        row_copy(p).start()
        meta_copy(p).start()

    fill(0, rows_in, 0)
    meta_in[0] = meta[me]
    in_here.wait()
    in_there.wait()
    out_here.wait()
    out_there.wait()

    def hidden(p):
        other_meta(p).start()

        @pl.loop(0, units // TILE)
        def _(n):
            cols = pl.ds(pl.multiple_of(n * TILE, TILE), TILE)
            pre = jnp.dot(rows_in[p], win[:, cols], preferred_element_type=jnp.float32)
            hid[p, 0:slot_rows, cols] = jax.nn.gelu(pre, approximate=True).astype(jnp.bfloat16)

        hid_copy(p).start()

    def mix(p):
        other_meta(p).wait()
        hid_copy(p).wait()
        here = jnp.transpose(meta_in[p])
        there = jnp.transpose(meta_other[p])
        lane = lax.broadcasted_iota(jnp.int32, (count, 2 * slot_rows), 1).astype(jnp.float32)
        weight = jnp.where(lane == here[:, 0:1], here[:, 1:2], 0.0) + jnp.where(
            lane == there[:, 0:1] + slot_rows, there[:, 1:2], 0.0
        )
        high = weight.astype(jnp.bfloat16)
        low = (weight - high.astype(jnp.float32)).astype(jnp.bfloat16)

        @pl.loop(0, units // TILE)
        def _(n):
            cols = pl.ds(pl.multiple_of(n * TILE, TILE), TILE)
            both = hid[p, :, cols]
            mixed[:, cols] = (
                jnp.dot(high, both, preferred_element_type=jnp.float32)
                + jnp.dot(low, both, preferred_element_type=jnp.float32)
            ).astype(jnp.bfloat16)

    hidden(0)
    mix(0)

    @pl.loop(0, half_width // TILE)
    def _(n):
        cols = pl.ds(pl.multiple_of(n * TILE, TILE), TILE)
        own[:, cols] = jnp.dot(mixed[...], wout[:, cols], preferred_element_type=jnp.float32)

    @pl.loop(1, experts)
    def _(p):
        meta_copy(p).wait()
        row_copy(p).wait()
        hidden(p)
        mix(p)
        if experts > slots:

            @pl.when(p > slots)
            def _():
                part_copy(p - slots).wait_send()

        @pl.loop(0, half_width // TILE)
        def _(n):
            cols = pl.ds(pl.multiple_of(n * TILE, TILE), TILE)
            part[lax.rem(p, slots), :, cols] = jnp.dot(
                mixed[...], wout[:, cols], preferred_element_type=jnp.float32
            ).astype(jnp.bfloat16)

        part_copy(p).start()

    @pl.loop(1, experts)
    def _(p):
        if experts > slots:

            @pl.when(p >= experts - slots)
            def _():
                part_copy(p).wait_send()
        else:
            part_copy(p).wait_send()
        part_copy(p).wait_recv()
        if experts > 4:
            own[...] += part_in[p].astype(jnp.float32)

    if experts > 4:
        guided[...] = own[...].astype(jnp.bfloat16)
    else:

        @pl.loop(0, half_width // TILE)
        def _(n):
            cols = pl.ds(pl.multiple_of(n * TILE, TILE), TILE)
            total = own[:, cols]
            for p in range(1, experts):
                total = total + part_in[p, :, cols].astype(jnp.float32)
            guided[:, cols] = total.astype(jnp.bfloat16)


def layer_2x2(
    tokens,
    routes,
    keep,
    router,
    w_in,
    w_out,
    guided,
    win,
    wout,
    meta,
    meta_in,
    meta_other,
    rows,
    rows_in,
    half_in,
    hid,
    mixed,
    own,
    late,
    part,
    part_in,
    weight_sem,
    half_send,
    half_recv,
    meta_send,
    meta_recv,
    row_send,
    row_recv,
    hid_send,
    hid_recv,
    mo_send,
    mo_recv,
    part_send,
    part_recv,
):
    experts = 4
    me = lax.axis_index("expert")
    branch = lax.axis_index("branch")
    other = 1 - branch
    count, width = tokens.shape
    half_units = w_in.shape[1]
    units = win.shape[1]
    half_width = guided.shape[1]
    slot_rows = rows.shape[1]
    half = width // 2
    quarter = half_width // 2
    span = quarter // PIECES

    barrier = pltpu.get_barrier_semaphore()
    for p in range(1, experts):
        pl.semaphore_signal(
            barrier, inc=1, device_id={"expert": me ^ p}, device_id_type=MESH
        )
    pl.semaphore_signal(barrier, inc=1, device_id={"branch": other}, device_id_type=MESH)
    pl.semaphore_wait(barrier, experts)

    def to_expert(p, source, target, send, recv):
        return pltpu.make_async_remote_copy(
            src_ref=source,
            dst_ref=target,
            send_sem=send,
            recv_sem=recv,
            device_id={"expert": me ^ p},
            device_id_type=MESH,
        )

    def to_core(source, target, send, recv):
        return pltpu.make_async_remote_copy(
            src_ref=source,
            dst_ref=target,
            send_sem=send,
            recv_sem=recv,
            device_id={"branch": other},
            device_id_type=MESH,
        )

    def raw(p):
        return to_expert(
            p,
            tokens.at[:, pl.ds((p - 1) * half, half)],
            half_in.at[p - 1],
            half_send.at[p - 1],
            half_recv.at[p - 1],
        )

    raw(1).start()
    raw(2).start()

    unit_at = pl.multiple_of(branch * half_units, 128)
    mine_at = pl.multiple_of(branch * half_width, 128)
    theirs_at = pl.multiple_of(other * half_width, 128)
    weights = [
        pltpu.make_async_copy(w_in, win.at[:, pl.ds(unit_at, half_units)], weight_sem.at[0]),
        to_core(w_in, win.at[:, pl.ds(unit_at, half_units)], weight_sem.at[2], weight_sem.at[3]),
        pltpu.make_async_copy(
            w_out.at[:, pl.ds(mine_at, half_width)],
            wout.at[pl.ds(unit_at, half_units), :],
            weight_sem.at[1],
        ),
        to_core(
            w_out.at[:, pl.ds(theirs_at, half_width)],
            wout.at[pl.ds(unit_at, half_units), :],
            weight_sem.at[4],
            weight_sem.at[5],
        ),
    ]
    for copy in weights:
        copy.start()

    find_slots(experts, branch, tokens, routes, keep, router, meta)

    def meta_copy(p):
        return to_expert(p, meta, meta_in.at[p], meta_send.at[p], meta_recv.at[p])

    for p in range(1, experts):
        meta_copy(p).start()

    def fill(slot_of, source, source_at, into, at, into_at):
        place = (
            lax.broadcasted_iota(jnp.int32, (slot_rows, count), 0).astype(jnp.float32) == slot_of
        )
        place = place.astype(jnp.float32).astype(jnp.bfloat16)

        @pl.loop(0, half // (2 * TILE))
        def _(n):
            off = n * 2 * TILE
            cols = pl.ds(pl.multiple_of(source_at + off, 2 * TILE), 2 * TILE)
            out = pl.ds(pl.multiple_of(into_at + off, 2 * TILE), 2 * TILE)
            into[at, :, out] = jnp.dot(
                place, source[:, cols], preferred_element_type=jnp.float32
            ).astype(jnp.bfloat16)

    def direct(p):
        cols = pl.ds((2 - p) * half, half)
        return to_expert(
            p, rows.at[p, :, cols], rows_in.at[p, :, cols], row_send.at[p], row_recv.at[p]
        )

    def forward(p):
        cols = pl.ds((2 - p) * half, half)
        return to_expert(
            p, rows.at[3, :, cols], rows_in.at[3, :, cols], row_send.at[p + 2], row_recv.at[p + 2]
        )

    for p in (1, 2):
        fill(meta[me ^ p, 0:1, :], tokens, (2 - p) * half, rows, p, (2 - p) * half)
    for p in (1, 2):
        raw(p).wait_send()
        direct(p).start()
    for h in range(2):
        fill(meta[me, 0:1, :], tokens, h * half, rows_in, 0, h * half)
    for p in range(1, experts):
        meta_copy(p).wait()
    for p in (1, 2):
        raw(p).wait_recv()
        q = 3 - p
        fill(meta_in[p, me ^ q, 0:1, :], half_in.at[p - 1], 0, rows, 3, (p - 1) * half)
        fill(meta_in[p, me, 0:1, :], half_in.at[p - 1], 0, rows_in, p, (p - 1) * half)
    meta_in[0] = meta[...]

    def other_meta(p):
        return to_core(meta_in.at[p, me], meta_other.at[p], mo_send.at[p], mo_recv.at[p])

    def hid_copy(p):
        return to_core(
            hid.at[p, pl.ds(0, slot_rows)],
            hid.at[p, pl.ds(slot_rows, slot_rows)],
            hid_send.at[p],
            hid_recv.at[p],
        )

    for p in range(experts):
        other_meta(p).start()

    def hidden(p):
        @pl.loop(0, units // TILE)
        def _(n):
            cols = pl.ds(pl.multiple_of(n * TILE, TILE), TILE)
            pre = jnp.dot(rows_in[p], win[:, cols], preferred_element_type=jnp.float32)
            hid[p, 0:slot_rows, cols] = jax.nn.gelu(pre, approximate=True).astype(jnp.bfloat16)

        hid_copy(p).start()

    def mix(p, into):
        other_meta(p).wait()
        here = jnp.transpose(meta_in[p, me])
        there = jnp.transpose(meta_other[p])
        lane = lax.broadcasted_iota(jnp.int32, (count, 2 * slot_rows), 1).astype(jnp.float32)
        weight = jnp.where(lane == here[:, 0:1], here[:, 1:2], 0.0) + jnp.where(
            lane == there[:, 0:1] + slot_rows, there[:, 1:2], 0.0
        )
        high = weight.astype(jnp.bfloat16)
        low = (weight - high.astype(jnp.float32)).astype(jnp.bfloat16)
        hid_copy(p).wait()

        @pl.loop(0, units // TILE)
        def _(n):
            cols = pl.ds(pl.multiple_of(n * TILE, TILE), TILE)
            both = hid[p, :, cols]
            mixed[into, :, cols] = (
                jnp.dot(high, both, preferred_element_type=jnp.float32)
                + jnp.dot(low, both, preferred_element_type=jnp.float32)
            ).astype(jnp.bfloat16)

    def output(of, side, piece, store):
        @pl.loop(0, span // TILE)
        def _(n):
            at = pl.multiple_of(piece * span + n * TILE, TILE)
            cols = pl.ds(pl.multiple_of(side * quarter + at, TILE), TILE)
            store(
                cols,
                pl.ds(at, TILE),
                jnp.dot(mixed[of], wout[:, cols], preferred_element_type=jnp.float32),
            )

    def keep_own(cols, _, value):
        own[:, cols] = value

    def to_part(p):
        def store(cols, _, value):
            part[p, :, cols] = value.astype(jnp.bfloat16)

        return store

    def to_late(index):
        def store(_, cols, value):
            late[index, :, cols] = value

        return store

    def part_copy(p, side, piece):
        index = (p - 1) * 2 * PIECES + side * PIECES + piece
        cols = pl.ds(side * quarter + piece * span, span)
        return to_expert(
            side + 1 if p == 3 else p,
            part.at[p, :, cols],
            part_in.at[p, :, cols],
            part_send.at[index],
            part_recv.at[index],
        )

    for copy in weights:
        copy.wait()
    hidden(0)
    forward(1).start()
    forward(2).start()
    mix(0, 0)
    for p in (1, 2):
        direct(p).wait()
        hidden(p)
    for p in (1, 2):
        mix(p, p)
        for c in range(PIECES):
            output(p, p - 1, c, to_part(p))
            part_copy(p, p - 1, c).start()
    for p in (1, 2):
        for c in range(PIECES):
            output(p, 2 - p, c, to_late(p - 1))
    for p in (1, 2):
        forward(p).wait()
    hidden(3)
    mix(3, 3)
    for c in range(PIECES):
        for side in range(2):
            output(3, side, c, to_part(3))
            part_copy(3, side, c).start()
    for side in range(2):
        for c in range(PIECES):
            output(0, side, c, keep_own)
    for c in range(PIECES):
        for side in range(2):
            p = 2 - side
            part_copy(3, side, c).wait()

            @pl.loop(0, span // TILE)
            def _(n):
                at = pl.multiple_of(c * span + n * TILE, TILE)
                cols = pl.ds(pl.multiple_of(side * quarter + at, TILE), TILE)
                part[p, :, cols] = (
                    late[p - 1, :, pl.ds(at, TILE)] + part_in[3, :, cols].astype(jnp.float32)
                ).astype(jnp.bfloat16)

            part_copy(p, side, c).start()
    for c in range(PIECES):
        for p in (1, 2):
            part_copy(p, p - 1, c).wait()
    for c in range(PIECES):
        for side in range(2):
            part_copy(2 - side, side, c).wait()

            @pl.loop(0, span // TILE)
            def _(n):
                at = side * quarter + c * span + n * TILE
                cols = pl.ds(pl.multiple_of(at, TILE), TILE)
                total = own[:, cols]
                for p in (1, 2):
                    total = total + part_in[p, :, cols].astype(jnp.float32)
                guided[:, cols] = total.astype(jnp.bfloat16)


def on_device(latents, routes, keep_mask, router, expert_in, expert_out):
    width = latents.shape[-1]
    tokens = latents.reshape(-1, width)
    count = tokens.shape[0]
    experts = lax.axis_size("expert")
    branches = lax.axis_size("branch")
    capacity = 5 * count * TOP // (4 * experts)
    slot_rows = -(-capacity // 16) * 16
    half_units = expert_in.shape[2]
    units = half_units * branches
    half_width = width // branches
    slots = min(experts, 4)
    routes = routes.reshape(count, TOP).T
    keep_mask = keep_mask.reshape(count, TOP).T
    bf16, f32 = jnp.bfloat16, jnp.float32
    vmem = pl.BlockSpec(memory_space=pltpu.VMEM)
    hbm = pl.BlockSpec(memory_space=pl.ANY)
    dma = pltpu.SemaphoreType.DMA
    if experts == 4:
        kernel = layer_2x2
        shapes = [
            ((width, units), bf16),
            ((units, half_width), bf16),
            ((experts, 8, count), f32),
            ((experts, experts, 8, count), f32),
            ((experts, 8, count), f32),
            ((experts, slot_rows, width), bf16),
            ((experts, slot_rows, width), bf16),
            ((2, count, width // 2), bf16),
            ((experts, 2 * slot_rows, units), bf16),
            ((experts, count, units), bf16),
            ((count, half_width), f32),
            ((2, count, half_width // 2), f32),
            ((experts, count, half_width), bf16),
            ((experts, count, half_width), bf16),
        ]
        semaphores = [6, 2, 2, 4, 4, 5, 5, 4, 4, 4, 4, 6 * PIECES, 6 * PIECES]
    else:
        kernel = functools.partial(layer, experts, slots)
        shapes = [
            ((width, units), bf16),
            ((units, half_width), bf16),
            ((experts, 8, count), f32),
            ((experts, 8, count), f32),
            ((experts, 8, count), f32),
            ((experts, slot_rows, width), bf16),
            ((experts, slot_rows, width), bf16),
            ((experts, 2 * slot_rows, units), bf16),
            ((count, units), bf16),
            ((count, half_width), f32),
            ((slots, count, half_width), bf16),
            ((experts, count, half_width), bf16),
        ]
        semaphores = [6] + [experts] * 10
    guided = pl.pallas_call(
        kernel,
        out_shape=jax.ShapeDtypeStruct((count, half_width), bf16),
        in_specs=[vmem, vmem, vmem, vmem, hbm, hbm],
        out_specs=vmem,
        scratch_shapes=[pltpu.VMEM(*s) for s in shapes] + [dma((s,)) for s in semaphores],
        compiler_params=pltpu.CompilerParams(
            collective_id=0, has_side_effects=True, vmem_limit_bytes=63 * 2**20
        ),
        cost_estimate=pl.CostEstimate(
            flops=13_000_000_000, bytes_accessed=20_000_000, transcendentals=1_000_000
        ),
    )(tokens, routes, keep_mask, router.T, expert_in[0], expert_out[0])
    return guided.reshape(latents.shape[1], latents.shape[2], half_width)


def solution(mesh):
    placed = (
        P("branch", ("member", "expert"), None, None),
        P("branch", ("member", "expert"), None, None),
        P("branch", ("member", "expert"), None, None),
        P(),
        P("expert", None, "branch"),
        P("expert", "branch", None),
    )
    return jax.shard_map(
        on_device,
        mesh=mesh,
        in_specs=placed,
        out_specs=P(("member", "expert"), None, "branch"),
        check_vma=False,
    )
```
